32 devices in a mesh: replica: 8 (over z, core), fsdp: 4 (over y, x).
Axes of the slice: x: 2, y: 2, z: 4, core: 2. Of those that a mesh axis runs over, the one named last changes fastest.
Arguments:
- tokens: bfloat16 [4096, 8192], P(('replica', 'fsdp')), may hold values from -6 to 6
- target: bfloat16 [4096, 512], P(('replica', 'fsdp')), may hold values from -6 to 6
- weight: bfloat16 [8, 8192, 512], P('replica', 'fsdp'), may hold values from -6 to 6
- pseudo: float32 [8, 8192, 512], P('replica', 'fsdp'), may hold values from -6 to 6
- global_frag: float32 [8192, 512], P('fsdp'), may hold values from -6 to 6
- momentum: float32 [8192, 512], P('fsdp'), may hold values from -2 to 2
Outputs:
- new_weight: bfloat16 [8, 8192, 512], P('replica', 'fsdp')
- residual: bfloat16 [4096, 512], P(('replica', 'fsdp'))
- new_global: float32 [8192, 512], P('fsdp')
- new_momentum: float32 [8192, 512], P('fsdp')
The draws below stay inside these ranges and needn't reach their ends.
All inputs are finite; a program needn't handle non-finite values.
Results may differ from the reference program's by a relative error of at most 0.013.
Values may be sent and summed in bfloat16 or wider, within the bound.
A program may use at most 128 MiB of HBM per device.

```python
import jax
import jax.numpy as jnp
from jax import lax

D = 8192
KV = 512
TOK_DEV = 128
TOK_ALL = 4096
N_REPLICA = 8
N_FSDP = 4


def level_of(rng, extent, cuts, smallest, high):
    def one(position, shards_of):
        draws = jax.random.uniform(jax.random.fold_in(jax.random.fold_in(rng, 6), position), (shards_of,), jnp.float32, smallest / len(cuts), high / len(cuts))
        return jnp.repeat(jnp.exp(draws), extent[position] // shards_of).reshape((-1,) + (1,) * (len(extent) - position - 1))

    gain = one(*cuts[0])
    for cut in cuts[1:]:
        gain = gain * one(*cut)
    return gain


def scatter_about(own_key, extent, width, bound, pieces=(), kind=jnp.bfloat16):
    array = width * jax.random.normal(own_key, extent, jnp.float32)
    if pieces:
        array = array * level_of(own_key, extent, pieces, -0.22, 0.18)
    return jnp.clip(array, -bound, bound).astype(kind)


def setup_inputs(seed: int = 0) -> dict:
    seeds = jax.random.split(jax.random.key(seed), 7)
    return {
        "tokens": scatter_about(seeds[0], (TOK_ALL, D), 1.0, 6.0, ((0, 32),)),
        "target": scatter_about(seeds[1], (TOK_ALL, KV), 1.0, 6.0, ((0, 32),)),
        "weight": scatter_about(seeds[2], (N_REPLICA, D, KV), 1.0, 6.0, ((0, 8), (1, 4))),
        "pseudo": scatter_about(seeds[3], (N_REPLICA, D, KV), 1.0, 6.0, ((0, 8), (1, 4)), jnp.float32),
        "global_frag": scatter_about(seeds[4], (D, KV), 1.0, 6.0, ((0, 4),), jnp.float32),
        "momentum": scatter_about(seeds[5], (D, KV), 0.3, 2.0, ((0, 4),), jnp.float32),
    }


inner_rate = 1.0
outer_rate = 0.7
nesterov_coef = 0.9
merge_share = 0.5


def reference(tokens, target, weight, pseudo, global_frag, momentum):
    key_scale = D ** -0.5
    replica_rows = TOK_DEV * N_FSDP
    block_width = D // N_FSDP

    def replica_step(operands):
        inputs_rep, target_rep, weight_rep = operands
        token_blocks = inputs_rep.reshape(replica_rows, N_FSDP, block_width).astype(jnp.float32)
        weight_blocks = weight_rep.reshape(N_FSDP, block_width, KV).astype(jnp.float32)
        partials = jnp.einsum('tfd,fdk->ftk', token_blocks, weight_blocks) * key_scale
        rounded = lax.optimization_barrier(partials.astype(jnp.bfloat16))
        keys = jnp.sum(rounded.astype(jnp.float32), axis=0)
        residual_rep = (keys - target_rep.astype(jnp.float32)).astype(jnp.bfloat16)
        gradient = lax.dot_general(inputs_rep, residual_rep, (((0,), (0,)), ((), ())),
                                   preferred_element_type=jnp.float32) * key_scale
        stepped = weight_rep.astype(jnp.float32) - inner_rate * gradient
        return stepped, residual_rep

    inputs_all = tokens.reshape(N_REPLICA, replica_rows, D)
    targets_all = target.reshape(N_REPLICA, replica_rows, KV)
    stepped, residual_all = lax.map(replica_step, (inputs_all, targets_all, weight))
    averaged = jnp.sum(pseudo, axis=0) / N_REPLICA
    new_momentum = nesterov_coef * momentum + averaged
    new_global = global_frag - outer_rate * (averaged + nesterov_coef * new_momentum)
    new_weight = (merge_share * stepped + (1.0 - merge_share) * new_global[None]).astype(jnp.bfloat16)
    return new_weight, residual_all.reshape(N_REPLICA * replica_rows, KV), new_global, new_momentum
```

```python
import functools

import jax
import jax.numpy as jnp
from jax import lax
from jax.experimental import pallas as pl
from jax.experimental.pallas import tpu as pltpu
from jax.sharding import PartitionSpec as P

inner_rate = 1.0
outer_rate = 0.7
nesterov_coef = 0.9
merge_share = 0.5

MESH = pl.DeviceIdType.MESH
F32 = jnp.float32
BF16 = jnp.bfloat16


def partner(me, step, n):
    if n & (n - 1):
        return lax.rem(me + step, n)
    total, bit = 0, 1
    while bit < n:
        total = total + lax.rem(lax.div(me, bit) + (step // bit) % 2, 2) * bit
        bit *= 2
    return total


def exchange(
    nr, nf, nt, nc, scale,
    tok, tgt, wt, ps, gf, mom,
    xt, ra, ng, nm, res, wv,
    x, s, rv, tv, own, pair, sbuf, inbuf, tot, gfv, momv,
    load_sem, xl_sem, own_sem,
    xs_sem, xr_sem, ss_sem, sr_sem, rs_sem, rr_sem,
    ps_sem, pr_sem, is_sem, ir_sem, os_sem, or_sem, ts_sem, tr_sem,
):
    rep, me = lax.axis_index("replica"), lax.axis_index("fsdp")
    core, pos = lax.rem(rep, 2), lax.div(rep, 2)
    other = 1 - core
    length = nr // 2
    mid = length // 2
    low = pos < mid
    inward = (jnp.where(low, pos + 1, pos - 1) * 2 + core, me)
    outward = (jnp.where(low, jnp.maximum(pos - 1, 0), jnp.minimum(pos + 1, length - 1)) * 2 + core, me)
    twin = (pos * 2 + other, me)
    is_mid = (pos == mid - 1) | (pos == mid)
    kind = jnp.where(is_mid, 1, 0)
    has_up = (pos > 0) & (pos < length - 1)
    th, dblk = x.shape[2], x.shape[3]
    rc = own.shape[1]
    half = nc * rc
    peers = [partner(me, d, nf) for d in range(1, nf)]

    barrier = pltpu.get_barrier_semaphore()
    greet = [(rep, q) for q in peers] + [
        twin,
        (lax.rem(pos + 1, length) * 2 + core, me),
        (lax.rem(pos + length - 1, length) * 2 + core, me),
    ]
    for device in greet:
        pl.semaphore_signal(barrier, inc=1, device_id=device, device_id_type=MESH)

    def local(src, dst, sem):
        copy = pltpu.make_async_copy(src, dst, sem)
        copy.start()
        return copy

    def remote(src, dst, send, recv, device):
        return pltpu.make_async_remote_copy(
            src_ref=src, dst_ref=dst, send_sem=send, recv_sem=recv, device_id=device, device_id_type=MESH
        )

    def rows(which, c):
        return pl.ds(pl.multiple_of(which * half + c * rc, rc), rc)

    def block(h, q):
        return tok.at[pl.ds(h * th, th), pl.ds(pl.multiple_of(q * dblk, 128), dblk)]

    own_copies = [local(ps.at[0, rows(core, c)], own.at[c], own_sem.at[c]) for c in range(nc)]
    x_copies = [local(block(h, me), x.at[h, me], xl_sem.at[h]) for h in range(nt)]
    w_copy = local(wt.at[0], wv, load_sem.at[0])
    t_copy = local(tgt, tv, load_sem.at[1])

    pl.semaphore_wait(barrier, len(greet))

    def pair_copy(c):
        return remote(ps.at[0, rows(other, c)], pair.at[c], ps_sem.at[c], pr_sem.at[c], twin)

    def x_copy(h, i):
        return remote(block(h, peers[i]), x.at[h, me], xs_sem.at[h, i], xr_sem.at[h, me], (rep, peers[i]))

    def s_copy(h, i):
        return remote(s.at[h, peers[i]], rv.at[h, me], ss_sem.at[h, i], sr_sem.at[h, me], (rep, peers[i]))

    def r_copy(h, i):
        return remote(ra.at[h, me], ra.at[h, me], rs_sem.at[h, i], rr_sem.at[h, me], (rep, peers[i]))

    def in_copy(c):
        return remote(sbuf.at[c], inbuf.at[kind, c], is_sem.at[c], ir_sem.at[kind, c], inward)

    def out_copy(c):
        return remote(tot.at[core, c], tot.at[core, c], os_sem.at[c], or_sem.at[c], outward)

    def twin_copy(c):
        return remote(tot.at[core, c], tot.at[core, c], ts_sem.at[c], tr_sem.at[c], twin)

    def arrive(ref, sem):
        remote(ref, ref, sem, sem, twin).wait_recv()

    for c in range(nc):
        pair_copy(c).start()
    for h in range(nt):
        for i in range(nf - 1):
            x_copy(h, i).start()
    gf_copy = local(gf, gfv, load_sem.at[2])
    mom_copy = local(mom, momv, load_sem.at[3])

    def chip_sum(c):
        own_copies[c].wait()
        pair_copy(c).wait_recv()
        return own[c] + pair[c]

    def up_end(c):
        sbuf[c] = chip_sum(c).astype(BF16)
        in_copy(c).start()

    def up_inner(c):
        total = chip_sum(c)
        arrive(inbuf.at[0, c], ir_sem.at[0, c])
        sbuf[c] = (total + inbuf[0, c].astype(F32)).astype(BF16)
        in_copy(c).start()

    def outer_step(which, c):
        at = rows(which, c)
        averaged = tot[which, c].astype(F32) / nr
        moved = nesterov_coef * momv[at, :] + averaged
        nm[at, :] = moved
        ng[at, :] = gfv[at, :] - outer_rate * (averaged + nesterov_coef * moved)

    def down(c):
        @pl.when(is_mid)
        def _():
            arrive(inbuf.at[1, c], ir_sem.at[1, c])
            tot[core, c] = (sbuf[c].astype(F32) + inbuf[1, c].astype(F32)).astype(BF16)

        @pl.when(jnp.logical_not(is_mid))
        def _():
            arrive(tot.at[core, c], or_sem.at[c])

        @pl.when(has_up)
        def _():
            out_copy(c).start()

        twin_copy(c).start()
        outer_step(core, c)

    def down_twin(c):
        arrive(tot.at[other, c], tr_sem.at[c])
        outer_step(other, c)

    def keys(h):
        x_copies[h].wait()
        for q in peers:
            arrive(x.at[h, q], xr_sem.at[h, q])
        block_h = x[h].reshape(nf * th, dblk)
        part = jnp.dot(block_h, wv[...], preferred_element_type=F32) * scale
        s[h] = part.astype(BF16).reshape(nf, th, part.shape[1])
        for i in range(nf - 1):
            s_copy(h, i).start()
        rv[h, me] = s[h, me]
        xt[:, h * nf * th:(h + 1) * nf * th] = block_h.T

    def error(h):
        for q in peers:
            arrive(rv.at[h, q], sr_sem.at[h, q])
        at = pl.ds(h * th, th)
        total = rv[h, 0].astype(F32)
        for f in range(1, nf):
            total = total + rv[h, f].astype(F32)
        err = (total - tv[at, :].astype(F32)).astype(BF16)
        ra[h, me] = err
        for i in range(nf - 1):
            r_copy(h, i).start()
        res[at, :] = err

    @pl.when(jnp.logical_not(has_up))
    def _():
        for c in range(nc):
            up_end(c)

    w_copy.wait()
    t_copy.wait()

    per = max(nc // nt, 1)
    for k in range(nc + 2):
        if k < nc:
            pl.when(has_up)(functools.partial(up_inner, k))
        if k == 1:
            gf_copy.wait()
            mom_copy.wait()
        if 1 <= k <= nc:
            down(k - 1)
        if k >= 2:
            down_twin(k - 2)
        if k >= 1 and k % per == 0 and k // per <= nt:
            keys(k // per - 1)
        if k >= 2 and (k - 1) % per == 0 and 1 <= (k - 1) // per <= nt:
            error((k - 1) // per - 1)

    for h in range(nt):
        for q in peers:
            arrive(ra.at[h, q], rr_sem.at[h, q])
    for c in range(nc):
        pair_copy(c).wait_send()
        in_copy(c).wait_send()
        twin_copy(c).wait_send()

    @pl.when(has_up)
    def _():
        for c in range(nc):
            out_copy(c).wait_send()

    for h in range(nt):
        for i in range(nf - 1):
            x_copy(h, i).wait_send()
            s_copy(h, i).wait_send()
            r_copy(h, i).wait_send()


def merge(nb, scale, xt, ra, ng, nm, res, wv, nw_out, res_out, ng_out, nm_out, nw, sems, w_sems):
    copies = [
        pltpu.make_async_copy(nm, nm_out, sems.at[0]),
        pltpu.make_async_copy(ng, ng_out, sems.at[1]),
        pltpu.make_async_copy(res, res_out, sems.at[2]),
    ]
    for copy in copies:
        copy.start()
    width = xt.shape[0] // nb
    errors = ra[...].reshape(xt.shape[1], ra.shape[-1])
    for b in range(nb):
        at = pl.ds(b * width, width)
        gradient = jnp.dot(xt[at, :], errors, preferred_element_type=F32) * scale
        stepped = wv[at, :].astype(F32) - inner_rate * gradient
        nw[at, :] = (merge_share * stepped + (1.0 - merge_share) * ng[at, :]).astype(BF16)
        copy = pltpu.make_async_copy(nw.at[at], nw_out.at[0, at], w_sems.at[b])
        copy.start()
        copies.append(copy)
    for copy in copies:
        copy.wait()


def solution(mesh):
    nr, nf = mesh.shape["replica"], mesh.shape["fsdp"]

    def shards(tokens, target, weight, pseudo, global_frag, momentum):
        t, width = tokens.shape
        _, dblk, kv = weight.shape
        scale = width ** (-0.5)
        nt = 4
        nc = 8
        nb = 8
        th, rc = t // nt, dblk // 2 // nc
        any_ = pl.BlockSpec(memory_space=pltpu.HBM)
        vmem = pl.BlockSpec(memory_space=pltpu.VMEM)
        dma = pltpu.SemaphoreType.DMA
        middle = pl.pallas_call(
            functools.partial(exchange, nr, nf, nt, nc, scale),
            out_shape=(
                pltpu.VMEM((dblk, nt * nf * th), BF16),
                pltpu.VMEM((nt, nf, th, kv), BF16),
                pltpu.VMEM((dblk, kv), F32),
                pltpu.VMEM((dblk, kv), F32),
                pltpu.VMEM((t, kv), BF16),
                pltpu.VMEM((dblk, kv), BF16),
            ),
            in_specs=[any_] * 6,
            out_specs=(vmem,) * 6,
            scratch_shapes=[
                pltpu.VMEM((nt, nf, th, dblk), BF16),
                pltpu.VMEM((nt, nf, th, kv), BF16),
                pltpu.VMEM((nt, nf, th, kv), BF16),
                pltpu.VMEM((t, kv), BF16),
                pltpu.VMEM((nc, rc, kv), F32),
                pltpu.VMEM((nc, rc, kv), F32),
                pltpu.VMEM((nc, rc, kv), BF16),
                pltpu.VMEM((2, nc, rc, kv), BF16),
                pltpu.VMEM((2, nc, rc, kv), BF16),
                pltpu.VMEM((dblk, kv), F32),
                pltpu.VMEM((dblk, kv), F32),
                dma((4,)), dma((nt,)), dma((nc,)),
                dma((nt, nf)), dma((nt, nf)), dma((nt, nf)), dma((nt, nf)), dma((nt, nf)), dma((nt, nf)),
                dma((nc,)), dma((nc,)), dma((nc,)), dma((2, nc)), dma((nc,)), dma((nc,)), dma((nc,)), dma((nc,)),
            ],
            compiler_params=pltpu.CompilerParams(
                collective_id=0, has_side_effects=True, vmem_limit_bytes=40 << 20
            ),
            name="exchange",
        )(tokens, target, weight, pseudo, global_frag, momentum)
        return pl.pallas_call(
            functools.partial(merge, nb, scale),
            out_shape=(
                jax.ShapeDtypeStruct((1, dblk, kv), BF16),
                jax.ShapeDtypeStruct((t, kv), BF16),
                jax.ShapeDtypeStruct((dblk, kv), F32),
                jax.ShapeDtypeStruct((dblk, kv), F32),
            ),
            in_specs=[vmem] * 6,
            out_specs=(any_,) * 4,
            scratch_shapes=[pltpu.VMEM((dblk, kv), BF16), dma((3,)), dma((nb,))],
            compiler_params=pltpu.CompilerParams(vmem_limit_bytes=40 << 20),
            name="merge",
        )(*middle)

    in_specs = (
        P(("replica", "fsdp"), None),
        P(("replica", "fsdp"), None),
        P("replica", "fsdp", None),
        P("replica", "fsdp", None),
        P("fsdp", None),
        P("fsdp", None),
    )
    out_specs = (
        P("replica", "fsdp", None),
        P(("replica", "fsdp"), None),
        P("fsdp", None),
        P("fsdp", None),
    )
    return jax.shard_map(shards, mesh=mesh, in_specs=in_specs, out_specs=out_specs, check_vma=False)
```

```python
import functools

import jax
import jax.numpy as jnp
from jax import lax
from jax.experimental import pallas as pl
from jax.experimental.pallas import tpu as pltpu
from jax.sharding import PartitionSpec as P

inner_rate = 1.0
outer_rate = 0.7
nesterov_coef = 0.9
merge_share = 0.5

MESH = pl.DeviceIdType.MESH
F32 = jnp.float32
BF16 = jnp.bfloat16


def partner(me, step, n):
    if n & (n - 1):
        return lax.rem(me + step, n)
    total, bit = 0, 1
    while bit < n:
        total = total + lax.rem(lax.div(me, bit) + (step // bit) % 2, 2) * bit
        bit *= 2
    return total


def exchange(
    nr, nf, nt, nc, scale,
    tok, tgt, wt, ps, gf, mom,
    xt, ra, ng, nm, res, wv,
    x, s, rv, tv, own, pair, sbuf, inbuf, tot, gfv, momv,
    load_sem, xl_sem, own_sem,
    xs_sem, xr_sem, ss_sem, sr_sem, rs_sem, rr_sem,
    ps_sem, pr_sem, is_sem, ir_sem, os_sem, or_sem, ts_sem, tr_sem,
):
    rep, me = lax.axis_index("replica"), lax.axis_index("fsdp")
    core, pos = lax.rem(rep, 2), lax.div(rep, 2)
    other = 1 - core
    length = nr // 2
    mid = length // 2
    low = pos < mid
    inward = (jnp.where(low, pos + 1, pos - 1) * 2 + core, me)
    outward = (jnp.where(low, jnp.maximum(pos - 1, 0), jnp.minimum(pos + 1, length - 1)) * 2 + core, me)
    twin = (pos * 2 + other, me)
    is_mid = (pos == mid - 1) | (pos == mid)
    kind = jnp.where(is_mid, 1, 0)
    has_up = (pos > 0) & (pos < length - 1)
    th, dblk = x.shape[2], x.shape[3]
    rc = own.shape[1]
    half = nc * rc
    peers = [partner(me, d, nf) for d in range(nf - 1, 0, -1)]

    barrier = pltpu.get_barrier_semaphore()
    greet = [(rep, q) for q in peers] + [
        twin,
        (lax.rem(pos + 1, length) * 2 + core, me),
        (lax.rem(pos + length - 1, length) * 2 + core, me),
    ]
    for device in greet:
        pl.semaphore_signal(barrier, inc=1, device_id=device, device_id_type=MESH)

    def local(src, dst, sem):
        copy = pltpu.make_async_copy(src, dst, sem)
        copy.start()
        return copy

    def remote(src, dst, send, recv, device):
        return pltpu.make_async_remote_copy(
            src_ref=src, dst_ref=dst, send_sem=send, recv_sem=recv, device_id=device, device_id_type=MESH
        )

    def rows(which, c):
        return pl.ds(pl.multiple_of(which * half + c * rc, rc), rc)

    def block(h, q):
        return tok.at[pl.ds(h * th, th), pl.ds(pl.multiple_of(q * dblk, 128), dblk)]

    own_copies = [local(ps.at[0, rows(core, c)], own.at[c], own_sem.at[c]) for c in range(nc)]
    x_copies = [local(block(h, me), x.at[h, me], xl_sem.at[h]) for h in range(nt)]
    w_copy = local(wt.at[0], wv, load_sem.at[0])
    t_copy = local(tgt, tv, load_sem.at[1])

    pl.semaphore_wait(barrier, len(greet))

    def pair_copy(c):
        return remote(ps.at[0, rows(other, c)], pair.at[c], ps_sem.at[c], pr_sem.at[c], twin)

    def x_copy(h, i):
        return remote(block(h, peers[i]), x.at[h, me], xs_sem.at[h, i], xr_sem.at[h, me], (rep, peers[i]))

    def s_copy(h, i):
        return remote(s.at[h, peers[i]], rv.at[h, me], ss_sem.at[h, i], sr_sem.at[h, me], (rep, peers[i]))

    def r_copy(h, i):
        return remote(ra.at[h, me], ra.at[h, me], rs_sem.at[h, i], rr_sem.at[h, me], (rep, peers[i]))

    def in_copy(c):
        return remote(sbuf.at[c], inbuf.at[kind, c], is_sem.at[c], ir_sem.at[kind, c], inward)

    def out_copy(c):
        return remote(tot.at[core, c], tot.at[core, c], os_sem.at[c], or_sem.at[c], outward)

    def twin_copy(c):
        return remote(tot.at[core, c], tot.at[core, c], ts_sem.at[c], tr_sem.at[c], twin)

    def arrive(ref, sem):
        remote(ref, ref, sem, sem, twin).wait_recv()

    for c in range(nc):
        pair_copy(c).start()
    for h in range(nt):
        for i in range(nf - 1):
            x_copy(h, i).start()
    gf_copy = local(gf, gfv, load_sem.at[2])
    mom_copy = local(mom, momv, load_sem.at[3])

    def chip_sum(c):
        own_copies[c].wait()
        pair_copy(c).wait_recv()
        return own[c] + pair[c]

    def up_end(c):
        sbuf[c] = chip_sum(c).astype(BF16)
        in_copy(c).start()

    def up_inner(c):
        total = chip_sum(c)
        arrive(inbuf.at[0, c], ir_sem.at[0, c])
        sbuf[c] = (total + inbuf[0, c].astype(F32)).astype(BF16)
        in_copy(c).start()

    def outer_step(which, c):
        at = rows(which, c)
        averaged = tot[which, c].astype(F32) / nr
        moved = nesterov_coef * momv[at, :] + averaged
        nm[at, :] = moved
        ng[at, :] = gfv[at, :] - outer_rate * (averaged + nesterov_coef * moved)

    def down(c):
        @pl.when(is_mid)
        def _():
            arrive(inbuf.at[1, c], ir_sem.at[1, c])
            tot[core, c] = (sbuf[c].astype(F32) + inbuf[1, c].astype(F32)).astype(BF16)

        @pl.when(jnp.logical_not(is_mid))
        def _():
            arrive(tot.at[core, c], or_sem.at[c])

        @pl.when(has_up)
        def _():
            out_copy(c).start()

        twin_copy(c).start()
        outer_step(core, c)

    def down_twin(c):
        arrive(tot.at[other, c], tr_sem.at[c])
        outer_step(other, c)

    def keys(h):
        x_copies[h].wait()
        for q in peers:
            arrive(x.at[h, q], xr_sem.at[h, q])
        block_h = x[h].reshape(nf * th, dblk)
        part = jnp.dot(block_h, wv[...], preferred_element_type=F32) * scale
        s[h] = part.astype(BF16).reshape(nf, th, part.shape[1])
        for i in range(nf - 1):
            s_copy(h, i).start()
        rv[h, me] = s[h, me]
        xt[:, h * nf * th:(h + 1) * nf * th] = block_h.T

    def error(h):
        for q in peers:
            arrive(rv.at[h, q], sr_sem.at[h, q])
        at = pl.ds(h * th, th)
        total = rv[h, 0].astype(F32)
        for f in range(1, nf):
            total = total + rv[h, f].astype(F32)
        err = (total - tv[at, :].astype(F32)).astype(BF16)
        ra[h, me] = err
        for i in range(nf - 1):
            r_copy(h, i).start()
        res[at, :] = err

    @pl.when(jnp.logical_not(has_up))
    def _():
        for c in range(nc):
            up_end(c)

    w_copy.wait()
    t_copy.wait()

    key_at, error_at = (3, 6), (5, 8)
    for k in range(nc + 2):
        if k < nc:
            pl.when(has_up)(functools.partial(up_inner, k))
        if k == 1:
            gf_copy.wait()
            mom_copy.wait()
        if 1 <= k <= nc:
            down(k - 1)
        if k >= 2:
            down_twin(k - 2)
        for h in range(nt):
            if k == key_at[h]:
                keys(h)
            if k == error_at[h]:
                error(h)

    for h in range(nt):
        for q in peers:
            arrive(ra.at[h, q], rr_sem.at[h, q])
    for c in range(nc):
        pair_copy(c).wait_send()
        in_copy(c).wait_send()
        twin_copy(c).wait_send()

    @pl.when(has_up)
    def _():
        for c in range(nc):
            out_copy(c).wait_send()

    for h in range(nt):
        for i in range(nf - 1):
            x_copy(h, i).wait_send()
            s_copy(h, i).wait_send()
            r_copy(h, i).wait_send()


def merge(nb, scale, xt, ra, ng, nm, res, wv, nw_out, res_out, ng_out, nm_out, nw, sems, w_sems, o_sems):
    copies = [
        pltpu.make_async_copy(res, res_out, sems.at[2]),
    ]
    for copy in copies:
        copy.start()
    width = xt.shape[0] // nb
    for b in range(nb):
        at = pl.ds(b * width, width)
        for i, (src, dst) in enumerate(((nm, nm_out), (ng, ng_out))):
            copy = pltpu.make_async_copy(src.at[at], dst.at[at], o_sems.at[i, b])
            copy.start()
            copies.append(copy)
    errors = ra[...].reshape(xt.shape[1], ra.shape[-1])
    for b in range(nb):
        at = pl.ds(b * width, width)
        gradient = jnp.dot(xt[at, :], errors, preferred_element_type=F32) * scale
        stepped = wv[at, :].astype(F32) - inner_rate * gradient
        nw[at, :] = (merge_share * stepped + (1.0 - merge_share) * ng[at, :]).astype(BF16)
        copy = pltpu.make_async_copy(nw.at[at], nw_out.at[0, at], w_sems.at[b])
        copy.start()
        copies.append(copy)
    for copy in copies:
        copy.wait()


def solution(mesh):
    nr, nf = mesh.shape["replica"], mesh.shape["fsdp"]

    def shards(tokens, target, weight, pseudo, global_frag, momentum):
        t, width = tokens.shape
        _, dblk, kv = weight.shape
        scale = width ** (-0.5)
        nt = 2
        nc = 8
        nb = 8
        th, rc = t // nt, dblk // 2 // nc
        any_ = pl.BlockSpec(memory_space=pltpu.HBM)
        vmem = pl.BlockSpec(memory_space=pltpu.VMEM)
        dma = pltpu.SemaphoreType.DMA
        middle = pl.pallas_call(
            functools.partial(exchange, nr, nf, nt, nc, scale),
            out_shape=(
                pltpu.VMEM((dblk, nt * nf * th), BF16),
                pltpu.VMEM((nt, nf, th, kv), BF16),
                pltpu.VMEM((dblk, kv), F32),
                pltpu.VMEM((dblk, kv), F32),
                pltpu.VMEM((t, kv), BF16),
                pltpu.VMEM((dblk, kv), BF16),
            ),
            in_specs=[any_] * 6,
            out_specs=(vmem,) * 6,
            scratch_shapes=[
                pltpu.VMEM((nt, nf, th, dblk), BF16),
                pltpu.VMEM((nt, nf, th, kv), BF16),
                pltpu.VMEM((nt, nf, th, kv), BF16),
                pltpu.VMEM((t, kv), BF16),
                pltpu.VMEM((nc, rc, kv), F32),
                pltpu.VMEM((nc, rc, kv), F32),
                pltpu.VMEM((nc, rc, kv), BF16),
                pltpu.VMEM((2, nc, rc, kv), BF16),
                pltpu.VMEM((2, nc, rc, kv), BF16),
                pltpu.VMEM((dblk, kv), F32),
                pltpu.VMEM((dblk, kv), F32),
                dma((4,)), dma((nt,)), dma((nc,)),
                dma((nt, nf)), dma((nt, nf)), dma((nt, nf)), dma((nt, nf)), dma((nt, nf)), dma((nt, nf)),
                dma((nc,)), dma((nc,)), dma((nc,)), dma((2, nc)), dma((nc,)), dma((nc,)), dma((nc,)), dma((nc,)),
            ],
            compiler_params=pltpu.CompilerParams(
                collective_id=0, has_side_effects=True, vmem_limit_bytes=40 << 20
            ),
            name="exchange",
        )(tokens, target, weight, pseudo, global_frag, momentum)
        return pl.pallas_call(
            functools.partial(merge, nb, scale),
            out_shape=(
                jax.ShapeDtypeStruct((1, dblk, kv), BF16),
                jax.ShapeDtypeStruct((t, kv), BF16),
                jax.ShapeDtypeStruct((dblk, kv), F32),
                jax.ShapeDtypeStruct((dblk, kv), F32),
            ),
            in_specs=[vmem] * 6,
            out_specs=(any_,) * 4,
            scratch_shapes=[pltpu.VMEM((dblk, kv), BF16), dma((3,)), dma((nb,)), dma((2, nb))],
            compiler_params=pltpu.CompilerParams(vmem_limit_bytes=40 << 20),
            name="merge",
        )(*middle)

    in_specs = (
        P(("replica", "fsdp"), None),
        P(("replica", "fsdp"), None),
        P("replica", "fsdp", None),
        P("replica", "fsdp", None),
        P("fsdp", None),
        P("fsdp", None),
    )
    out_specs = (
        P("replica", "fsdp", None),
        P(("replica", "fsdp"), None),
        P("fsdp", None),
        P("fsdp", None),
    )
    return jax.shard_map(shards, mesh=mesh, in_specs=in_specs, out_specs=out_specs, check_vma=False)
```

```python
import functools

import jax
import jax.numpy as jnp
from jax import lax
from jax.experimental import pallas as pl
from jax.experimental.pallas import tpu as pltpu
from jax.sharding import PartitionSpec as P

inner_rate = 1.0
outer_rate = 0.7
nesterov_coef = 0.9
merge_share = 0.5

MESH = pl.DeviceIdType.MESH
F32 = jnp.float32
BF16 = jnp.bfloat16


def partner(me, step, n):
    if n & (n - 1):
        return lax.rem(me + step, n)
    total, bit = 0, 1
    while bit < n:
        total = total + lax.rem(lax.div(me, bit) + (step // bit) % 2, 2) * bit
        bit *= 2
    return total


def exchange(
    nr, nf, parts, nc, scale,
    tok, tgt, wt, ps, gf, mom,
    xt, ra, ng, nm, res, wv,
    x, s, rv, tv, own, pair, sbuf, inbuf, tot, gfv, momv,
    load_sem, xl_sem, own_sem,
    xs_sem, xr_sem, ss_sem, sr_sem, rs_sem, rr_sem,
    ps_sem, pr_sem, is_sem, ir_sem, os_sem, or_sem, ts_sem, tr_sem,
):
    rep, me = lax.axis_index("replica"), lax.axis_index("fsdp")
    nt = len(parts)
    core, pos = lax.rem(rep, 2), lax.div(rep, 2)
    other = 1 - core
    length = nr // 2
    mid = length // 2
    low = pos < mid
    inward = (jnp.where(low, pos + 1, pos - 1) * 2 + core, me)
    outward = (jnp.where(low, jnp.maximum(pos - 1, 0), jnp.minimum(pos + 1, length - 1)) * 2 + core, me)
    twin = (pos * 2 + other, me)
    is_mid = (pos == mid - 1) | (pos == mid)
    kind = jnp.where(is_mid, 1, 0)
    has_up = (pos > 0) & (pos < length - 1)
    dblk = x.shape[1]
    rc = own.shape[1]
    half = nc * rc
    peers = [partner(me, d, nf) for d in range(nf - 1, 0, -1)]

    barrier = pltpu.get_barrier_semaphore()
    greet = [(rep, q) for q in peers] + [
        twin,
        (lax.rem(pos + 1, length) * 2 + core, me),
        (lax.rem(pos + length - 1, length) * 2 + core, me),
    ]
    for device in greet:
        pl.semaphore_signal(barrier, inc=1, device_id=device, device_id_type=MESH)

    def local(src, dst, sem):
        copy = pltpu.make_async_copy(src, dst, sem)
        copy.start()
        return copy

    def remote(src, dst, send, recv, device):
        return pltpu.make_async_remote_copy(
            src_ref=src, dst_ref=dst, send_sem=send, recv_sem=recv, device_id=device, device_id_type=MESH
        )

    def rows(which, c):
        return pl.ds(pl.multiple_of(which * half + c * rc, rc), rc)

    first = [sum(parts[:h]) for h in range(nt)]

    def own_rows(h):
        return pl.ds(first[h], parts[h])

    def at_rows(h, q):
        return pl.ds(pl.multiple_of(nf * first[h] + q * parts[h], 16), parts[h])

    def all_rows(h):
        return pl.ds(nf * first[h], nf * parts[h])

    def block(h, q):
        return tok.at[own_rows(h), pl.ds(pl.multiple_of(q * dblk, 128), dblk)]

    own_copies = [local(ps.at[0, rows(core, c)], own.at[c], own_sem.at[c]) for c in range(nc)]
    x_copies = [local(block(h, me), x.at[at_rows(h, me)], xl_sem.at[h]) for h in range(nt)]
    w_copy = local(wt.at[0], wv, load_sem.at[0])
    t_copy = local(tgt, tv, load_sem.at[1])

    pl.semaphore_wait(barrier, len(greet))

    def pair_copy(c):
        return remote(ps.at[0, rows(other, c)], pair.at[c], ps_sem.at[c], pr_sem.at[c], twin)

    def x_copy(h, i):
        return remote(block(h, peers[i]), x.at[at_rows(h, me)], xs_sem.at[h, i], xr_sem.at[h, me], (rep, peers[i]))

    def s_copy(h, i):
        return remote(s.at[at_rows(h, peers[i])], rv.at[at_rows(h, me)], ss_sem.at[h, i], sr_sem.at[h, me], (rep, peers[i]))

    def r_copy(h, i):
        return remote(ra.at[at_rows(h, me)], ra.at[at_rows(h, me)], rs_sem.at[h, i], rr_sem.at[h, me], (rep, peers[i]))

    def in_copy(c):
        return remote(sbuf.at[c], inbuf.at[kind, c], is_sem.at[c], ir_sem.at[kind, c], inward)

    def out_copy(c):
        return remote(tot.at[core, c], tot.at[core, c], os_sem.at[c], or_sem.at[c], outward)

    def twin_copy(c):
        return remote(tot.at[core, c], tot.at[core, c], ts_sem.at[c], tr_sem.at[c], twin)

    def arrive(ref, sem):
        remote(ref, ref, sem, sem, twin).wait_recv()

    for c in range(nc):
        pair_copy(c).start()
    for h in range(nt):
        for i in range(nf - 1):
            x_copy(h, i).start()
    gf_copy = local(gf, gfv, load_sem.at[2])
    mom_copy = local(mom, momv, load_sem.at[3])

    def chip_sum(c):
        own_copies[c].wait()
        pair_copy(c).wait_recv()
        return own[c] + pair[c]

    def up_end(c):
        sbuf[c] = chip_sum(c).astype(BF16)
        in_copy(c).start()

    def up_inner(c):
        total = chip_sum(c)
        arrive(inbuf.at[0, c], ir_sem.at[0, c])
        sbuf[c] = (total + inbuf[0, c].astype(F32)).astype(BF16)
        in_copy(c).start()

    def outer_step(which, c):
        at = rows(which, c)
        averaged = tot[which, c].astype(F32) / nr
        moved = nesterov_coef * momv[at, :] + averaged
        nm[at, :] = moved
        ng[at, :] = gfv[at, :] - outer_rate * (averaged + nesterov_coef * moved)

    def down(c):
        @pl.when(is_mid)
        def _():
            arrive(inbuf.at[1, c], ir_sem.at[1, c])
            tot[core, c] = (sbuf[c].astype(F32) + inbuf[1, c].astype(F32)).astype(BF16)

        @pl.when(jnp.logical_not(is_mid))
        def _():
            arrive(tot.at[core, c], or_sem.at[c])

        @pl.when(has_up)
        def _():
            out_copy(c).start()

        twin_copy(c).start()
        outer_step(core, c)

    def down_twin(c):
        arrive(tot.at[other, c], tr_sem.at[c])
        outer_step(other, c)

    def keys(h):
        x_copies[h].wait()
        for q in peers:
            arrive(x.at[at_rows(h, q)], xr_sem.at[h, q])
        block_h = x[all_rows(h), :]
        part = jnp.dot(block_h, wv[...], preferred_element_type=F32) * scale
        s[all_rows(h), :] = part.astype(BF16)
        for i in range(nf - 1):
            s_copy(h, i).start()
        rv[at_rows(h, me), :] = s[at_rows(h, me), :]
        xt[:, all_rows(h)] = block_h.T

    def error(h):
        for q in peers:
            arrive(rv.at[at_rows(h, q)], sr_sem.at[h, q])
        at = own_rows(h)
        total = rv[at_rows(h, 0), :].astype(F32)
        for f in range(1, nf):
            total = total + rv[at_rows(h, f), :].astype(F32)
        err = (total - tv[at, :].astype(F32)).astype(BF16)
        ra[at_rows(h, me), :] = err
        for i in range(nf - 1):
            r_copy(h, i).start()
        res[at, :] = err

    @pl.when(jnp.logical_not(has_up))
    def _():
        for c in range(nc):
            up_end(c)

    w_copy.wait()
    t_copy.wait()

    key_at, error_at = (5, 6), (7, 8)
    for k in range(nc + 2):
        if k < nc:
            pl.when(has_up)(functools.partial(up_inner, k))
        if k == 1:
            gf_copy.wait()
            mom_copy.wait()
        if 1 <= k <= nc:
            down(k - 1)
        if k >= 2:
            down_twin(k - 2)
        for h in range(nt):
            if k == key_at[h]:
                keys(h)
            if k == error_at[h]:
                error(h)

    for h in range(nt):
        for q in peers:
            arrive(ra.at[at_rows(h, q)], rr_sem.at[h, q])
    for c in range(nc):
        pair_copy(c).wait_send()
        in_copy(c).wait_send()
        twin_copy(c).wait_send()

    @pl.when(has_up)
    def _():
        for c in range(nc):
            out_copy(c).wait_send()

    for h in range(nt):
        for i in range(nf - 1):
            x_copy(h, i).wait_send()
            s_copy(h, i).wait_send()
            r_copy(h, i).wait_send()


def merge(nb, scale, xt, ra, ng, nm, res, wv, nw_out, res_out, ng_out, nm_out, nw, sems, w_sems, o_sems):
    copies = [
        pltpu.make_async_copy(res, res_out, sems.at[2]),
    ]
    for copy in copies:
        copy.start()
    width = xt.shape[0] // nb
    for b in range(nb):
        at = pl.ds(b * width, width)
        for i, (src, dst) in enumerate(((nm, nm_out), (ng, ng_out))):
            copy = pltpu.make_async_copy(src.at[at], dst.at[at], o_sems.at[i, b])
            copy.start()
            copies.append(copy)
    errors = ra[...]
    for b in range(nb):
        at = pl.ds(b * width, width)
        gradient = jnp.dot(xt[at, :], errors, preferred_element_type=F32) * scale
        stepped = wv[at, :].astype(F32) - inner_rate * gradient
        nw[at, :] = (merge_share * stepped + (1.0 - merge_share) * ng[at, :]).astype(BF16)
        copy = pltpu.make_async_copy(nw.at[at], nw_out.at[0, at], w_sems.at[b])
        copy.start()
        copies.append(copy)
    for copy in copies:
        copy.wait()


def solution(mesh):
    nr, nf = mesh.shape["replica"], mesh.shape["fsdp"]

    def shards(tokens, target, weight, pseudo, global_frag, momentum):
        t, width = tokens.shape
        _, dblk, kv = weight.shape
        scale = width ** (-0.5)
        parts = (t * 3 // 4, t - t * 3 // 4)
        nt = len(parts)
        nc = 8
        nb = 8
        rc = dblk // 2 // nc
        any_ = pl.BlockSpec(memory_space=pltpu.HBM)
        vmem = pl.BlockSpec(memory_space=pltpu.VMEM)
        dma = pltpu.SemaphoreType.DMA
        middle = pl.pallas_call(
            functools.partial(exchange, nr, nf, parts, nc, scale),
            out_shape=(
                pltpu.VMEM((dblk, nf * t), BF16),
                pltpu.VMEM((nf * t, kv), BF16),
                pltpu.VMEM((dblk, kv), F32),
                pltpu.VMEM((dblk, kv), F32),
                pltpu.VMEM((t, kv), BF16),
                pltpu.VMEM((dblk, kv), BF16),
            ),
            in_specs=[any_] * 6,
            out_specs=(vmem,) * 6,
            scratch_shapes=[
                pltpu.VMEM((nf * t, dblk), BF16),
                pltpu.VMEM((nf * t, kv), BF16),
                pltpu.VMEM((nf * t, kv), BF16),
                pltpu.VMEM((t, kv), BF16),
                pltpu.VMEM((nc, rc, kv), F32),
                pltpu.VMEM((nc, rc, kv), F32),
                pltpu.VMEM((nc, rc, kv), BF16),
                pltpu.VMEM((2, nc, rc, kv), BF16),
                pltpu.VMEM((2, nc, rc, kv), BF16),
                pltpu.VMEM((dblk, kv), F32),
                pltpu.VMEM((dblk, kv), F32),
                dma((4,)), dma((nt,)), dma((nc,)),
                dma((nt, nf)), dma((nt, nf)), dma((nt, nf)), dma((nt, nf)), dma((nt, nf)), dma((nt, nf)),
                dma((nc,)), dma((nc,)), dma((nc,)), dma((2, nc)), dma((nc,)), dma((nc,)), dma((nc,)), dma((nc,)),
            ],
            compiler_params=pltpu.CompilerParams(
                collective_id=0, has_side_effects=True, vmem_limit_bytes=40 << 20
            ),
            name="exchange",
        )(tokens, target, weight, pseudo, global_frag, momentum)
        return pl.pallas_call(
            functools.partial(merge, nb, scale),
            out_shape=(
                jax.ShapeDtypeStruct((1, dblk, kv), BF16),
                jax.ShapeDtypeStruct((t, kv), BF16),
                jax.ShapeDtypeStruct((dblk, kv), F32),
                jax.ShapeDtypeStruct((dblk, kv), F32),
            ),
            in_specs=[vmem] * 6,
            out_specs=(any_,) * 4,
            scratch_shapes=[pltpu.VMEM((dblk, kv), BF16), dma((3,)), dma((nb,)), dma((2, nb))],
            compiler_params=pltpu.CompilerParams(vmem_limit_bytes=40 << 20),
            name="merge",
        )(*middle)

    in_specs = (
        P(("replica", "fsdp"), None),
        P(("replica", "fsdp"), None),
        P("replica", "fsdp", None),
        P("replica", "fsdp", None),
        P("fsdp", None),
        P("fsdp", None),
    )
    out_specs = (
        P("replica", "fsdp", None),
        P(("replica", "fsdp"), None),
        P("fsdp", None),
        P("fsdp", None),
    )
    return jax.shard_map(shards, mesh=mesh, in_specs=in_specs, out_specs=out_specs, check_vma=False)
```
